32 devices in a mesh: seq: 16 (over z, y, core), tp: 2 (over x).
Axes of the slice: x: 2, y: 2, z: 4, core: 2. Of those that a mesh axis runs over, the one named last changes fastest.
Arguments:
- qkv_se: bfloat16 [8192, 3, 4096], P('seq', None, 'tp'), may hold values from -6 to 6
- residual: bfloat16 [8192, 4096], P('seq', 'tp'), may hold values from -108 to 108
- taps_se: bfloat16 [256, 7], P('tp'), may hold values from -2 to 2
- skip_se: bfloat16 [4096], P('tp'), may hold values from 0.5 to 1.5
- w_out: bfloat16 [4096, 4096], P('tp', 'seq'), may hold values from -0.125 to 0.125
- norm_gain: bfloat16 [4096], replicated, may hold values from 0.5 to 1.5
- w_in: bfloat16 [4096, 3, 4096], P('seq', None, 'tp'), may hold values from -0.09375 to 0.09375
- taps_mr: bfloat16 [256, 128], P('tp'), may hold values from -0.5 to 0.5
- skip_mr: bfloat16 [4096], P('tp'), may hold values from 0.5 to 1.5
Outputs:
- mixed: bfloat16 [8192, 4096], P('seq', 'tp')
The draws below stay inside these ranges and needn't reach their ends.
All inputs are finite; a program needn't handle non-finite values.
Results may differ from the reference program's by a relative error of at most 0.0085.
Values may be sent and summed in bfloat16 or wider, within the bound.
A program may use at most 128 MiB of HBM per device.

```python
import math
import jax
import jax.numpy as jnp
from jax import lax

D = 4096
GROUP = 16
SE_TAPS = 7
MR_TAPS = 128
TOKENS = 8192
GROUPS = 256


def draw_residual(key, part):
    key_base, key_rows, key_cols = jax.random.split(key, 3)
    row_scale = jnp.exp(jax.random.uniform(key_rows, (TOKENS, 1), jnp.float32, math.log(0.3), math.log(3.0)))
    column_index = jnp.arange(D, dtype=jnp.float32)[None, :] / D
    col_scale = jnp.exp(jax.random.uniform(key_cols, (1, D), jnp.float32, math.log(0.5), math.log(2.0)))
    col_scale = col_scale * jnp.exp(math.log(3.0) * column_index)
    base = jnp.clip(jax.random.normal(key_base, (TOKENS, D), jnp.float32), -6.0, 6.0)
    return (base * row_scale * col_scale).astype(jnp.bfloat16)


def spiked(drawn, own_key, source, target, blocks, factor):
    def block_of(position):
        return (jnp.arange(drawn.shape[position]) // (drawn.shape[position] // blocks)).reshape((-1,) + (1,) * (drawn.ndim - 1 - position))

    one_side = jax.random.permutation(own_key, blocks)[block_of(target)]
    other_side = (block_of(target) + blocks // 2) % blocks
    return jnp.where((block_of(source) == one_side) | (block_of(source) == other_side), factor * drawn, drawn)


def steps_of(stream_key, dims, cuts, least, top_value):
    loudness, own = 1.0, jax.random.fold_in(stream_key, 6)
    for position, shards_of in cuts:
        draws = jnp.exp(jax.random.uniform(jax.random.fold_in(own, position), (shards_of,), jnp.float32, least / len(cuts), top_value / len(cuts)))
        loudness = loudness * jnp.repeat(draws, dims[position] // shards_of).reshape([-1 if axis == position else 1 for axis in range(len(dims))])
    return loudness


def scatter_about(rng, extent, deviation, most, shards=(), kind=jnp.bfloat16):
    array = jax.random.normal(rng, extent, jnp.float32) * deviation
    if len(shards) > 0:
        array = steps_of(rng, extent, shards, -0.22, 0.18) * array
    return jnp.clip(array, min=-most, max=most).astype(kind)


def gaussian_with(own_key, dims, deviation, bound, pieces, heavy, held_as=jnp.bfloat16):
    array = deviation * jax.random.normal(own_key, dims, jnp.float32)
    if pieces:
        array = array * steps_of(own_key, dims, pieces, -0.22, 0.18)
    return jnp.clip(spiked(array, jax.random.fold_in(own_key, 3), *heavy), -bound, bound).astype(held_as)


def setup_inputs(seed: int = 0) -> dict:
    seeds = jax.random.split(jax.random.key(seed), 10)
    return {
        "qkv_se": scatter_about(seeds[0], (TOKENS, 3, D), 1.0, 6.0, ((0, 16), (2, 2))),
        "residual": draw_residual(jax.random.fold_in(seeds[9], 71), 0),
        "taps_se": scatter_about(seeds[2], (GROUPS, SE_TAPS), SE_TAPS ** -0.5, 2.0, ((0, 2),)),
        "skip_se": jnp.clip(0.5 + 1.0 * jax.random.uniform(seeds[3], (D,), jnp.float32) ** steps_of(seeds[3], (D,), ((0, 2),), -0.2, 0.2), 0.5, 1.5).astype(jnp.bfloat16),
        "w_out": gaussian_with(seeds[4], (D, D), D ** -0.5, 0.125, ((0, 2), (1, 16)), (0, 1, 16, 2.0)),
        "norm_gain": jnp.clip(1.0 + 0.1 * jax.random.normal(seeds[5], (D,), jnp.float32), 0.5, 1.5).astype(jnp.bfloat16),
        "w_in": scatter_about(seeds[6], (D, 3, D), D ** -0.5, 0.09375, ((0, 16), (2, 2))),
        "taps_mr": scatter_about(seeds[7], (GROUPS, MR_TAPS), MR_TAPS ** -0.5, 0.5, ((0, 2),)),
        "skip_mr": jnp.clip(0.5 + 1.0 * jax.random.uniform(seeds[8], (D,), jnp.float32) ** steps_of(seeds[8], (D,), ((0, 2),), -0.2, 0.2), 0.5, 1.5).astype(jnp.bfloat16),
    }


norm_eps = 1e-05

def short_conv(values, taps):
    per_channel = jnp.repeat(taps.astype(jnp.float32), GROUP, axis=0)
    wide = values.astype(jnp.float32)
    padded = jnp.concatenate([jnp.zeros((SE_TAPS - 1, wide.shape[1]), jnp.float32), wide], axis=0)
    total = jnp.zeros_like(wide)
    for tap_index in range(SE_TAPS):
        begin = SE_TAPS - 1 - tap_index
        total = total + per_channel[:, tap_index] * padded[begin:begin + wide.shape[0]]
    return total

def toeplitz_pair(taps):
    offsets = jnp.arange(MR_TAPS)[:, None] - jnp.arange(MR_TAPS)[None, :]
    table = taps[:, jnp.remainder(offsets, MR_TAPS)]
    lower = jnp.where(offsets >= 0, table, jnp.zeros_like(table))
    upper = jnp.where(offsets < 0, table, jnp.zeros_like(table))
    return (lower, upper)

def long_conv(values, taps):
    count = values.shape[0]
    chans = values.shape[1]
    lower, upper = toeplitz_pair(taps.astype(jnp.float32))
    blocks = values.astype(jnp.float32).reshape(count // MR_TAPS, MR_TAPS, chans // GROUP, GROUP)
    earlier = jnp.concatenate([jnp.zeros_like(blocks[:1]), blocks[:-1]], axis=0)
    result = jnp.einsum('gts,bsgc->btgc', lower, blocks) + jnp.einsum('gts,bsgc->btgc', upper, earlier)
    return result.reshape(count, chans)

def reference(qkv_se, residual, taps_se, skip_se, w_out, norm_gain, w_in, taps_mr, skip_mr):
    query_se = qkv_se[:, 0].astype(jnp.float32)
    u_se = (qkv_se[:, 1].astype(jnp.float32) * qkv_se[:, 2].astype(jnp.float32)).astype(jnp.bfloat16)
    conv_se = short_conv(u_se, taps_se)
    y_se = (query_se * (conv_se + skip_se.astype(jnp.float32) * u_se.astype(jnp.float32))).astype(jnp.bfloat16)
    stream = residual.astype(jnp.float32) + jnp.dot(y_se, w_out, preferred_element_type=jnp.float32)
    scale = lax.rsqrt(lax.optimization_barrier(jnp.mean(stream * stream, axis=1, keepdims=True)) + norm_eps)
    normed = (stream * scale * norm_gain.astype(jnp.float32)).astype(jnp.bfloat16)
    proj = jnp.dot(normed, w_in.reshape(D, 3 * D), preferred_element_type=jnp.float32).reshape(TOKENS, 3, D)
    query_mr = proj[:, 0]
    u_mr = (proj[:, 1] * proj[:, 2]).astype(jnp.bfloat16)
    conv_mr = long_conv(u_mr, taps_mr)
    return (query_mr * (conv_mr + skip_mr.astype(jnp.float32) * u_mr.astype(jnp.float32))).astype(jnp.bfloat16)
```

```python
import functools
import jax
import jax.numpy as jnp
from jax import lax
from jax.experimental import pallas as pl
from jax.experimental.pallas import tpu as pltpu
from jax.sharding import PartitionSpec as P

GROUP = 16
SE_TAPS = 7
MR_TAPS = 128


norm_eps = 1e-05


def shifted(block, axis, distance):
    devices = range(lax.axis_size(axis))
    route = [(i - distance, i) for i in devices if i - distance in devices]
    return lax.ppermute(block, axis, route)


LANES = 128
PER_TILE = LANES // GROUP


def table_kernel(taps_ref, out_ref):
    lag = lax.broadcasted_iota(jnp.int32, (MR_TAPS, MR_TAPS), 0) - lax.broadcasted_iota(
        jnp.int32, (MR_TAPS, MR_TAPS), 1
    )
    for g in range(PER_TILE):
        row = jnp.broadcast_to(taps_ref[g : g + 1, :], (MR_TAPS, MR_TAPS))
        table = pltpu.roll(row, 0, 1, stride=1, stride_axis=0)
        rows = pl.ds(g * MR_TAPS, MR_TAPS)
        out_ref[rows, :MR_TAPS] = jnp.where(lag >= 0, table, 0.0).astype(jnp.bfloat16)
        out_ref[rows, MR_TAPS:] = jnp.where(lag < 0, table, 0.0).astype(jnp.bfloat16)


def filter_tables(taps):
    groups = taps.shape[0]
    wide = taps.astype(jnp.float32)
    flipped = jnp.concatenate([wide[:, :1], wide[:, :0:-1]], axis=1)
    return pl.pallas_call(
        table_kernel,
        grid=(groups // PER_TILE,),
        in_specs=[pl.BlockSpec((PER_TILE, MR_TAPS), lambda i: (i, 0))],
        out_specs=pl.BlockSpec((PER_TILE * MR_TAPS, 2 * MR_TAPS), lambda i: (i, 0)),
        out_shape=jax.ShapeDtypeStruct((groups * MR_TAPS, 2 * MR_TAPS), jnp.bfloat16),
        cost_estimate=pl.CostEstimate(
            flops=groups * MR_TAPS * MR_TAPS * 16, bytes_accessed=groups * MR_TAPS * MR_TAPS * 4, transcendentals=0
        ),
    )(flipped)


def conv_kernel(blocks, table_ref, u_ref, tail_ref, query_ref, skip_ref, out_ref):
    u = u_ref[...]
    now = jnp.concatenate([u[b * MR_TAPS : (b + 1) * MR_TAPS] for b in range(blocks)], axis=1)
    before = jnp.concatenate([tail_ref[...], now[:, : (blocks - 1) * LANES]], axis=1)
    rhs = jnp.concatenate([now, before], axis=0)
    owner = lax.rem(lax.broadcasted_iota(jnp.int32, (MR_TAPS, blocks * LANES), 1), LANES) // GROUP
    total = None
    for g in range(PER_TILE):
        part = jnp.dot(
            table_ref[g * MR_TAPS : (g + 1) * MR_TAPS, :], rhs, preferred_element_type=jnp.float32
        )
        total = part if total is None else jnp.where(owner == g, part, total)
    for b in range(blocks):
        rows = slice(b * MR_TAPS, (b + 1) * MR_TAPS)
        direct = skip_ref[...].astype(jnp.float32) * u[rows].astype(jnp.float32)
        conv = total[:, b * LANES : (b + 1) * LANES]
        out_ref[rows, :] = (query_ref[rows, :] * (conv + direct)).astype(jnp.bfloat16)


def long_conv(tables, u_mr, tail, query, skip):
    rows, width = u_mr.shape
    tile = lambda i: (0, i)
    return pl.pallas_call(
        functools.partial(conv_kernel, rows // MR_TAPS),
        grid=(width // LANES,),
        in_specs=[
            pl.BlockSpec((PER_TILE * MR_TAPS, 2 * MR_TAPS), lambda i: (i, 0)),
            pl.BlockSpec((rows, LANES), tile),
            pl.BlockSpec((MR_TAPS, LANES), tile),
            pl.BlockSpec((rows, LANES), tile),
            pl.BlockSpec((1, LANES), tile),
        ],
        out_specs=pl.BlockSpec((rows, LANES), tile),
        out_shape=jax.ShapeDtypeStruct((rows, width), jnp.bfloat16),
        compiler_params=pltpu.CompilerParams(vmem_limit_bytes=32 * 1024 * 1024),
        cost_estimate=pl.CostEstimate(
            flops=rows * width * 4096, bytes_accessed=rows * width * 16, transcendentals=0
        ),
    )(tables, u_mr, tail, query, skip.reshape(1, width))


def swap(block):
    return lax.ppermute(block, "tp", [(0, 1), (1, 0)])


def sum_over_tp(partial):
    if lax.axis_size("tp") != 2:
        return lax.psum_scatter(partial, "tp", scatter_dimension=1, tiled=True)
    half = partial.shape[1] // 2
    first = lax.axis_index("tp") == 0
    low, high = partial[:, :half], partial[:, half:]
    sent = jnp.where(first, high, low).astype(jnp.bfloat16)
    return jnp.where(first, low, high) + swap(sent).astype(jnp.float32)


def gather_tp(block):
    if lax.axis_size("tp") != 2:
        return lax.all_gather(block, "tp", axis=1, tiled=True)
    first = lax.axis_index("tp") == 0
    other = swap(block)
    return jnp.concatenate(
        [jnp.where(first, block, other), jnp.where(first, other, block)], axis=1
    )


def project_out(y_se, w_out):
    return jnp.dot(
        y_se, lax.all_gather(w_out, "seq", axis=1, tiled=True), preferred_element_type=jnp.float32
    )


def per_device(qkv_se, residual, taps_se, skip_se, w_out, norm_gain, w_in, taps_mr, skip_mr):
    row_count = qkv_se.shape[0]
    chan_width = qkv_se.shape[2]
    query_se = qkv_se[:, 0].astype(jnp.float32)
    u_se = (qkv_se[:, 1].astype(jnp.float32) * qkv_se[:, 2].astype(jnp.float32)).astype(
        jnp.bfloat16
    )
    incoming_se = shifted(u_se[row_count - (SE_TAPS - 1) :], "seq", 1)
    extended = jnp.concatenate([incoming_se, u_se], axis=0).astype(jnp.float32)
    per_channel = jnp.repeat(taps_se.astype(jnp.float32), GROUP, axis=0)
    conv_se = jnp.zeros((row_count, chan_width), jnp.float32)
    for tap_index in range(SE_TAPS):
        begin = SE_TAPS - 1 - tap_index
        conv_se = conv_se + per_channel[:, tap_index] * extended[begin : begin + row_count]
    y_se = (query_se * (conv_se + skip_se.astype(jnp.float32) * u_se.astype(jnp.float32))).astype(
        jnp.bfloat16
    )
    gain_full = norm_gain.astype(jnp.float32)
    partial_out = project_out(y_se, w_out)
    share = sum_over_tp(partial_out)
    stream = residual.astype(jnp.float32) + share
    squares = lax.psum(jnp.sum(stream * stream, axis=1), "tp")
    scale = lax.rsqrt(squares / (chan_width * lax.axis_size("tp")) + norm_eps)
    my_gain = lax.dynamic_slice_in_dim(gain_full, lax.axis_index("tp") * chan_width, chan_width, 0)
    normed = (stream * scale[:, None] * my_gain).astype(jnp.bfloat16)
    gathered = gather_tp(normed)
    piece = lax.all_gather(w_in, "seq", axis=0, tiled=True)
    flat_piece = piece.reshape(piece.shape[0], 3 * chan_width)
    proj = jnp.dot(gathered, flat_piece, preferred_element_type=jnp.float32).reshape(
        row_count, 3, chan_width
    )
    query_mr = proj[:, 0]
    u_mr = (proj[:, 1] * proj[:, 2]).astype(jnp.bfloat16)
    tail = shifted(u_mr[row_count - MR_TAPS :], "seq", 1)
    return long_conv(filter_tables(taps_mr), u_mr, tail, query_mr, skip_mr)


def solution(mesh):
    placed = (
        P("seq", None, "tp"),
        P("seq", "tp"),
        P("tp", None),
        P("tp"),
        P("tp", "seq"),
        P(),
        P("seq", None, "tp"),
        P("tp", None),
        P("tp"),
    )
    return jax.shard_map(
        per_device, mesh=mesh, in_specs=placed, out_specs=P("seq", "tp"), check_vma=False
    )
```

```python
import functools
import jax
import jax.numpy as jnp
from jax import lax
from jax.experimental import pallas as pl
from jax.experimental.pallas import tpu as pltpu
from jax.sharding import PartitionSpec as P

GROUP = 16
SE_TAPS = 7
MR_TAPS = 128


norm_eps = 1e-05


def shifted(block, axis, distance):
    devices = range(lax.axis_size(axis))
    route = [(i - distance, i) for i in devices if i - distance in devices]
    return lax.ppermute(block, axis, route)


LANES = 128
PER_TILE = LANES // GROUP


def table_kernel(taps_ref, out_ref):
    lag = lax.broadcasted_iota(jnp.int32, (MR_TAPS, MR_TAPS), 0) - lax.broadcasted_iota(
        jnp.int32, (MR_TAPS, MR_TAPS), 1
    )
    for g in range(PER_TILE):
        row = jnp.broadcast_to(taps_ref[g : g + 1, :], (MR_TAPS, MR_TAPS))
        table = pltpu.roll(row, 0, 1, stride=1, stride_axis=0)
        rows = pl.ds(g * MR_TAPS, MR_TAPS)
        out_ref[rows, :MR_TAPS] = jnp.where(lag >= 0, table, 0.0).astype(jnp.bfloat16)
        out_ref[rows, MR_TAPS:] = jnp.where(lag < 0, table, 0.0).astype(jnp.bfloat16)


def filter_tables(taps):
    groups = taps.shape[0]
    wide = taps.astype(jnp.float32)
    flipped = jnp.concatenate([wide[:, :1], wide[:, :0:-1]], axis=1)
    return pl.pallas_call(
        table_kernel,
        grid=(groups // PER_TILE,),
        in_specs=[pl.BlockSpec((PER_TILE, MR_TAPS), lambda i: (i, 0))],
        out_specs=pl.BlockSpec((PER_TILE * MR_TAPS, 2 * MR_TAPS), lambda i: (i, 0)),
        out_shape=jax.ShapeDtypeStruct((groups * MR_TAPS, 2 * MR_TAPS), jnp.bfloat16),
        cost_estimate=pl.CostEstimate(
            flops=groups * MR_TAPS * MR_TAPS * 16, bytes_accessed=groups * MR_TAPS * MR_TAPS * 4, transcendentals=0
        ),
    )(flipped)


def conv_kernel(blocks, table_ref, u_ref, tail_ref, skip_ref, out_ref):
    u = u_ref[...]
    now = jnp.concatenate([u[b * MR_TAPS : (b + 1) * MR_TAPS] for b in range(blocks)], axis=1)
    before = jnp.concatenate([tail_ref[...], now[:, : (blocks - 1) * LANES]], axis=1)
    rhs = jnp.concatenate([now, before], axis=0)
    owner = lax.rem(lax.broadcasted_iota(jnp.int32, (MR_TAPS, blocks * LANES), 1), LANES) // GROUP
    total = None
    for g in range(PER_TILE):
        part = jnp.dot(
            table_ref[g * MR_TAPS : (g + 1) * MR_TAPS, :], rhs, preferred_element_type=jnp.float32
        )
        total = part if total is None else jnp.where(owner == g, part, total)
    for b in range(blocks):
        rows = slice(b * MR_TAPS, (b + 1) * MR_TAPS)
        direct = skip_ref[...].astype(jnp.float32) * u[rows].astype(jnp.float32)
        conv = total[:, b * LANES : (b + 1) * LANES]
        out_ref[rows, :] = conv + direct


def long_conv(tables, u_mr, tail, skip):
    rows, width = u_mr.shape
    tile = lambda i: (0, i)
    return pl.pallas_call(
        functools.partial(conv_kernel, rows // MR_TAPS),
        grid=(width // LANES,),
        in_specs=[
            pl.BlockSpec((PER_TILE * MR_TAPS, 2 * MR_TAPS), lambda i: (i, 0)),
            pl.BlockSpec((rows, LANES), tile),
            pl.BlockSpec((MR_TAPS, LANES), tile),
            pl.BlockSpec((1, LANES), tile),
        ],
        out_specs=pl.BlockSpec((rows, LANES), tile),
        out_shape=jax.ShapeDtypeStruct((rows, width), jnp.float32),
        compiler_params=pltpu.CompilerParams(vmem_limit_bytes=32 * 1024 * 1024),
        cost_estimate=pl.CostEstimate(
            flops=rows * width * 4096, bytes_accessed=rows * width * 16, transcendentals=0
        ),
    )(tables, u_mr, tail, skip.reshape(1, width))


def swap(block):
    return lax.ppermute(block, "tp", [(0, 1), (1, 0)])


def sum_over_tp(partial):
    if lax.axis_size("tp") != 2:
        return lax.psum_scatter(partial, "tp", scatter_dimension=1, tiled=True)
    half = partial.shape[1] // 2
    first = lax.axis_index("tp") == 0
    low, high = partial[:, :half], partial[:, half:]
    sent = jnp.where(first, high, low).astype(jnp.bfloat16)
    return jnp.where(first, low, high) + swap(sent).astype(jnp.float32)


def gather_tp(block):
    if lax.axis_size("tp") != 2:
        return lax.all_gather(block, "tp", axis=1, tiled=True)
    first = lax.axis_index("tp") == 0
    other = swap(block)
    return jnp.concatenate(
        [jnp.where(first, block, other), jnp.where(first, other, block)], axis=1
    )


def out_kernel(y_ref, w_ref, out_ref):
    out_ref[...] = jnp.dot(y_ref[...], w_ref[0], preferred_element_type=jnp.float32)


def project_out(y_se, shards):
    count, depth, width = shards.shape
    rows = y_se.shape[0]
    return pl.pallas_call(
        out_kernel,
        grid=(count,),
        in_specs=[
            pl.BlockSpec((rows, depth), lambda i: (0, 0)),
            pl.BlockSpec((1, depth, width), lambda i: (i, 0, 0)),
        ],
        out_specs=pl.BlockSpec((rows, width), lambda i: (0, i)),
        out_shape=jax.ShapeDtypeStruct((rows, count * width), jnp.float32),
        compiler_params=pltpu.CompilerParams(vmem_limit_bytes=32 * 1024 * 1024),
        cost_estimate=pl.CostEstimate(
            flops=2 * rows * depth * count * width,
            bytes_accessed=2 * count * depth * width + 4 * rows * count * width,
            transcendentals=0,
        ),
    )(y_se, shards)


def per_device(qkv_se, residual, taps_se, skip_se, w_out, norm_gain, w_in, taps_mr, skip_mr):
    row_count = qkv_se.shape[0]
    chan_width = qkv_se.shape[2]
    query_se = qkv_se[:, 0].astype(jnp.float32)
    u_se = (qkv_se[:, 1].astype(jnp.float32) * qkv_se[:, 2].astype(jnp.float32)).astype(
        jnp.bfloat16
    )
    incoming_se = shifted(u_se[row_count - (SE_TAPS - 1) :], "seq", 1)
    extended = jnp.concatenate([incoming_se, u_se], axis=0).astype(jnp.float32)
    per_channel = jnp.repeat(taps_se.astype(jnp.float32), GROUP, axis=0)
    conv_se = jnp.zeros((row_count, chan_width), jnp.float32)
    for tap_index in range(SE_TAPS):
        begin = SE_TAPS - 1 - tap_index
        conv_se = conv_se + per_channel[:, tap_index] * extended[begin : begin + row_count]
    y_se = (query_se * (conv_se + skip_se.astype(jnp.float32) * u_se.astype(jnp.float32))).astype(
        jnp.bfloat16
    )
    gain_full = norm_gain.astype(jnp.float32)
    out_full = lax.all_gather(w_out, "seq", axis=0, tiled=False)
    w_query, w_key, w_value, out_full, y_se = lax.optimization_barrier(
        (w_in[:, 0], w_in[:, 1], w_in[:, 2], out_full, y_se)
    )
    key_full = lax.all_gather(w_key, "seq", axis=0, tiled=True)
    partial_out = project_out(y_se, out_full)
    share = sum_over_tp(partial_out)
    w_value, key_full, share = lax.optimization_barrier((w_value, key_full, share))
    value_full = lax.all_gather(w_value, "seq", axis=0, tiled=True)
    stream = residual.astype(jnp.float32) + share
    squares = lax.psum(jnp.sum(stream * stream, axis=1), "tp")
    scale = lax.rsqrt(squares / (chan_width * lax.axis_size("tp")) + norm_eps)
    my_gain = lax.dynamic_slice_in_dim(gain_full, lax.axis_index("tp") * chan_width, chan_width, 0)
    normed = (stream * scale[:, None] * my_gain).astype(jnp.bfloat16)
    gathered = gather_tp(normed)
    key_mr = jnp.dot(gathered, key_full, preferred_element_type=jnp.float32)
    w_query, value_full, key_mr = lax.optimization_barrier((w_query, value_full, key_mr))
    query_full = lax.all_gather(w_query, "seq", axis=0, tiled=True)
    value_mr = jnp.dot(gathered, value_full, preferred_element_type=jnp.float32)
    u_mr = (key_mr * value_mr).astype(jnp.bfloat16)
    tail = shifted(u_mr[row_count - MR_TAPS :], "seq", 1)
    gate = long_conv(filter_tables(taps_mr), u_mr, tail, skip_mr)
    query_mr = jnp.dot(gathered, query_full, preferred_element_type=jnp.float32)
    return (query_mr * gate).astype(jnp.bfloat16)


def solution(mesh):
    placed = (
        P("seq", None, "tp"),
        P("seq", "tp"),
        P("tp", None),
        P("tp"),
        P("tp", "seq"),
        P(),
        P("seq", None, "tp"),
        P("tp", None),
        P("tp"),
    )
    return jax.shard_map(
        per_device, mesh=mesh, in_specs=placed, out_specs=P("seq", "tp"), check_vma=False
    )
```
